512 devices in a mesh: row: 16 (over x, y), col: 32 (over z, core).
Axes of the slice: x: 4, y: 4, z: 16, core: 2. Of those that a mesh axis runs over, the one named last changes fastest.
Arguments:
- diag_tile: bfloat16 [1024, 1024], P('row'), as said below
- row_u: bfloat16 [16, 1024, 256], P('row', 'col'), may hold values from -6 to 6
- row_v: bfloat16 [16, 1024, 256], P('row', 'col'), may hold values from -0.1875 to 0.1875
- col_u: bfloat16 [32, 1024, 256], P('col', 'row'), may hold values from -6 to 6
- col_v: bfloat16 [32, 1024, 256], P('col', 'row'), may hold values from -0.1875 to 0.1875
- tile_u: bfloat16 [16, 32, 1024, 256], P('row', 'col'), may hold values from -6 to 6
- tile_v: bfloat16 [16, 32, 1024, 256], P('row', 'col'), may hold values from -0.375 to 0.375
- omega: bfloat16 [1024, 128], replicated, may hold values from -6 to 6
- row_rank: int32 [16], P('row'), may hold values from 96 to 256, as said below
- col_rank: int32 [32], P('col'), may hold values from 96 to 256, as said below
- tile_rank: int32 [16, 32], P('row', 'col'), may hold values from 96 to 256, as said below
- keep_rank: int32 [16, 32], P('row', 'col'), may hold values from 32 to 128, as said below
Outputs:
- diag_factor: float32 [1024, 1024], P('row')
- row_solved: bfloat16 [16, 1024, 256], P('row', 'col')
- col_solved: bfloat16 [32, 1024, 256], P('col', 'row')
- new_u: bfloat16 [16, 32, 1024, 128], P('row', 'col')
- new_v: bfloat16 [16, 32, 1024, 128], P('row', 'col')
The draws below stay inside these ranges and needn't reach their ends.
Inputs may be any that keep to these rules, and one draw needn't show every extreme that they name: `row_rank`: columns of a panel factor at or past its rank hold arbitrary values; some tile has rank exactly 256. `col_rank`: as for row_rank. `tile_rank`: as for row_rank. `keep_rank`: some tile keeps exactly 128. `diag_tile`: symmetric positive definite covariance tile.
All inputs are finite; a program needn't handle non-finite values.
Results may differ from the reference program's by a relative error of at most 0.011.
Values may be sent and summed in bfloat16 or wider, within the bound.
No kernel may reach another device: no remote copies, remote signals or barrier semaphores. Data moves between devices by JAX's collectives and lax.ppermute only.
A program may use at most 128 MiB of HBM per device.

```python
import jax
import jax.numpy as jnp
from jax import lax

NB = 1024
KMAX = 256
KEEP = 128
NR = 16
NC = 32


def ranked_draw(key, count, lowest, highest):
    values = jax.random.randint(key, (count,), lowest, highest + 1, dtype=jnp.int32)
    where = jax.random.randint(jax.random.fold_in(key, 7), (), 0, count, dtype=jnp.int32)
    return values.at[where].set(highest)


def draw_diag_tile(key, part):
    points = jax.random.uniform(jax.random.fold_in(key, 11), (NB, 2), jnp.float32)
    delta_x = points[:, 0][:, None] - points[:, 0][None, :]
    delta_y = points[:, 1][:, None] - points[:, 1][None, :]
    distance = jnp.sqrt(delta_x * delta_x + delta_y * delta_y)
    length = 0.1
    nugget = 0.5
    covariance = jnp.exp(-distance / length) + nugget * jnp.eye(NB, dtype=jnp.float32)
    return covariance.astype(jnp.bfloat16)


def draw_row_rank(key, part):
    return ranked_draw(jax.random.fold_in(key, 21), NR, 3 * KMAX // 8, KMAX)


def draw_col_rank(key, part):
    return ranked_draw(jax.random.fold_in(key, 22), NC, 3 * KMAX // 8, KMAX)


def draw_tile_rank(key, part):
    return ranked_draw(jax.random.fold_in(key, 23), NR * NC, 3 * KMAX // 8, KMAX).reshape((NR, NC))


def draw_keep_rank(key, part):
    return ranked_draw(jax.random.fold_in(key, 24), NR * NC, KEEP // 4, KEEP).reshape((NR, NC))


def levels(own_key, shape, split, smallest, high):
    def one(position, blocks):
        draws = jax.random.uniform(jax.random.fold_in(jax.random.fold_in(own_key, 6), position), (blocks,), jnp.float32, smallest / len(split), high / len(split))
        return jnp.repeat(jnp.exp(draws), shape[position] // blocks).reshape((-1,) + (1,) * (len(shape) - position - 1))

    gain = one(*split[0])
    for cut in split[1:]:
        gain = gain * one(*cut)
    return gain


def bell_draw(rng, shape, deviation, most, cuts=(), kind=jnp.bfloat16):
    entries = deviation * jax.random.normal(rng, shape, jnp.float32)
    if cuts:
        entries = entries * levels(rng, shape, cuts, -0.22, 0.18)
    return jnp.clip(entries, -most, most).astype(kind)


def setup_inputs(seed: int = 0) -> dict:
    keys = jax.random.split(jax.random.key(seed), 13)
    return {
        "diag_tile": draw_diag_tile(jax.random.fold_in(keys[12], 71), 0),
        "row_u": bell_draw(keys[1], (NR, NB, KMAX), 1.0, 6.0, ((0, 16), (1, 32))),
        "row_v": bell_draw(keys[2], (NR, NB, KMAX), NB ** -0.5, 0.1875, ((0, 16), (1, 32))),
        "col_u": bell_draw(keys[3], (NC, NB, KMAX), 1.0, 6.0, ((0, 32), (1, 16))),
        "col_v": bell_draw(keys[4], (NC, NB, KMAX), NB ** -0.5, 0.1875, ((0, 32), (1, 16))),
        "tile_u": bell_draw(keys[5], (NR, NC, NB, KMAX), 1.0, 6.0, ((0, 16), (1, 32))),
        "tile_v": bell_draw(keys[6], (NR, NC, NB, KMAX), KMAX ** -0.5, 0.375, ((0, 16), (1, 32))),
        "omega": bell_draw(keys[7], (NB, KEEP), 1.0, 6.0),
        "row_rank": draw_row_rank(jax.random.fold_in(keys[12], 71), 0),
        "col_rank": draw_col_rank(jax.random.fold_in(keys[12], 71), 0),
        "tile_rank": draw_tile_rank(jax.random.fold_in(keys[12], 71), 0),
        "keep_rank": draw_keep_rank(jax.random.fold_in(keys[12], 71), 0),
    }


HIGH = lax.Precision.HIGHEST

def cut_columns(values, ranks):
    width = values.shape[-1]
    live = jnp.arange(width, dtype=jnp.int32) < ranks[..., None, None]
    return jnp.where(live, values, jnp.zeros_like(values))

def recompress(tu, tv, trank, krank, u_row, couple, u_col, omega):
    width = tu.shape[-1]
    keep = omega.shape[-1]
    live = (jnp.arange(width, dtype=jnp.int32) < trank)[None, :]
    u_tile = jnp.where(live, tu, jnp.zeros_like(tu)).astype(jnp.float32)
    v_tile = jnp.where(live, tv, jnp.zeros_like(tv)).astype(jnp.float32)
    along = jnp.dot(u_row.astype(jnp.float32), couple, precision=HIGH)
    left = jnp.concatenate([u_tile, along], axis=1)
    right = jnp.concatenate([v_tile, -u_col.astype(jnp.float32)], axis=1)
    kept = jnp.arange(keep, dtype=jnp.int32) < krank
    sketch = jnp.where(kept[None, :], omega.astype(jnp.float32), jnp.float32(0.0))
    inner = jnp.einsum('nk,nr->kr', right, sketch, precision=HIGH)
    sample = jnp.dot(left, inner, precision=HIGH)
    gram = jnp.einsum('nr,ns->rs', sample, sample, precision=HIGH)
    gram = gram + jnp.diag(jnp.where(kept, jnp.float32(0.0), jnp.float32(1.0)))
    lower = jnp.linalg.cholesky(gram)
    basis_t = lax.linalg.triangular_solve(lower, sample.T, left_side=True, lower=True)
    basis = basis_t.T
    proj = jnp.einsum('nk,nr->kr', left, basis, precision=HIGH)
    weights = jnp.dot(right, proj, precision=HIGH)
    scale = jnp.float32(tu.shape[0]) ** 0.5
    return ((basis * scale).astype(jnp.bfloat16), weights.astype(jnp.bfloat16))

def reference(diag_tile, row_u, row_v, col_u, col_v, tile_u, tile_v, omega, row_rank, col_rank, tile_rank, keep_rank):
    factor = jnp.linalg.cholesky(diag_tile.astype(jnp.float32))
    order = factor.shape[0]
    inverse = lax.linalg.triangular_solve(factor, jnp.eye(order, dtype=jnp.float32), left_side=True, lower=True)
    inverse = inverse.astype(jnp.bfloat16).astype(jnp.float32)
    ru = cut_columns(row_u, row_rank)
    rv = cut_columns(row_v, row_rank)
    cu = cut_columns(col_u, col_rank)
    cv = cut_columns(col_v, col_rank)
    row_solved = jnp.einsum('mn,ink->imk', inverse, rv.astype(jnp.float32), precision=HIGH).astype(jnp.bfloat16)
    col_solved = jnp.einsum('mn,ink->imk', inverse, cv.astype(jnp.float32), precision=HIGH).astype(jnp.bfloat16)
    rows_all = tile_u.shape[0]
    cols_all = tile_u.shape[1]
    count = rows_all * cols_all
    flat_u = tile_u.reshape((count,) + tile_u.shape[2:])
    flat_v = tile_v.reshape((count,) + tile_v.shape[2:])
    flat_t = tile_rank.reshape((count,))
    flat_k = keep_rank.reshape((count,))
    index = jnp.arange(count, dtype=jnp.int32)

    def one_tile(items):
        tu, tv, trank, krank, where = items
        i_row = where // cols_all
        j_col = where % cols_all
        w_row = row_solved[i_row].astype(jnp.float32)
        w_col = col_solved[j_col].astype(jnp.float32)
        couple = jnp.einsum('np,nq->pq', w_row, w_col, precision=HIGH)
        return recompress(tu, tv, trank, krank, ru[i_row], couple, cu[j_col], omega)
    new_u, new_v = lax.map(one_tile, (flat_u, flat_v, flat_t, flat_k, index))
    new_u = new_u.reshape((rows_all, cols_all) + new_u.shape[1:])
    new_v = new_v.reshape((rows_all, cols_all) + new_v.shape[1:])
    return (factor, row_solved, col_solved, new_u, new_v)
```

```python
import jax, jax.numpy as jnp
from jax import lax
from jax.sharding import PartitionSpec as P
from jax.experimental import pallas as pl
from jax.experimental.pallas import tpu as pltpu
F32=jnp.float32; BF=jnp.bfloat16
G=8

def lane(x,c): return jnp.broadcast_to(x[:,c:c+1],(8,128))
def sub(x,s): return jnp.broadcast_to(x[s:s+1,:],(8,128))

def factor(S):
    row=lax.broadcasted_iota(jnp.int32,(8,128),0); col=lax.broadcasted_iota(jnp.int32,(8,128),1)
    W=[jnp.where(col==row+8*g,F32(1),F32(0)) for g in range(16)]
    S=list(S)
    for p in range(16):
        C={g:[lane(S[g],8*p+j) for j in range(8)] for g in range(p,16)}
        a=[[sub(C[p][j],i) if i>=j else None for j in range(8)] for i in range(8)]
        B=[sub(S[p],j) for j in range(8)]; V=[sub(W[p],j) for j in range(8)]
        r=[None]*8
        l=[[None]*8 for _ in range(8)]
        for j in range(8):
            r[j]=lax.rsqrt(a[j][j])
            for i in range(j+1,8): l[i][j]=a[i][j]*r[j]
            B[j]=B[j]*r[j]; V[j]=V[j]*r[j]
            for i in range(j+1,8):
                for k in range(j+1,i+1): a[i][k]=a[i][k]-l[i][j]*l[k][j]
                B[i]=B[i]-l[i][j]*B[j]; V[i]=V[i]-l[i][j]*V[j]
        S[p]=B[0]; W[p]=V[0]
        for j in range(1,8):
            S[p]=jnp.where(row==j,B[j],S[p]); W[p]=jnp.where(row==j,V[j],W[p])
        if p<15:
            X=list(B); Y=list(V)
            for j in range(7,-1,-1):
                X[j]=X[j]*r[j]; Y[j]=Y[j]*r[j]
                for i in range(j):
                    X[i]=X[i]-l[j][i]*X[j]; Y[i]=Y[i]-l[j][i]*Y[j]
            for g in range(p+1,16):
                t=[C[g][j]*X[j] for j in range(8)]; u=[C[g][j]*Y[j] for j in range(8)]
                S[g]=S[g]-(((t[0]+t[1])+(t[2]+t[3]))+((t[4]+t[5])+(t[6]+t[7])))
                W[g]=W[g]-(((u[0]+u[1])+(u[2]+u[3]))+((u[4]+u[5])+(u[6]+u[7])))
    return S,W

def split(x):
    h=x.astype(BF); return h,(x-h.astype(F32)).astype(BF)
def dotg(a,b,ca,cb): return lax.dot_general(a,b,(((ca,),(cb,)),((),())),preferred_element_type=F32)
def dot3(a,b,ca,cb):
    ah,al=split(a); bh,bl=split(b)
    return dotg(ah,bh,ca,cb)+(dotg(ah,bl,ca,cb)+dotg(al,bh,ca,cb))

def chol_kernel(who,mine,other,l_ref,m_ref,buf,lcol):
    N=1024; nb=8
    strip=who[0]; b=lax.shift_right_logical(strip,1)
    c=lax.bitwise_and(who[1],1)*32
    for s in range(16):
        buf[pl.ds(pl.multiple_of(64*s+c,32),32),:]=mine[s].astype(F32)
        buf[pl.ds(pl.multiple_of(64*s+32-c,32),32),:]=other[s].astype(F32)
    l_ref[...]=jnp.zeros_like(l_ref)
    m_ref[...]=jnp.zeros_like(m_ref)
    def step(k,_):
        k0=pl.multiple_of(k*128,128)
        blk=pl.ds(k0,128)
        S,W=factor([buf[pl.ds(pl.multiple_of(k0+8*g,8),8),blk] for g in range(16)])
        row=lax.broadcasted_iota(jnp.int32,(8,128),0); col=lax.broadcasted_iota(jnp.int32,(8,128),1)
        R=jnp.concatenate([jnp.where(col>=row+8*g,S[g],F32(0)) for g in range(16)],0)
        M=jnp.concatenate(W,0)
        @pl.when(k==b)
        def _():
            lcol[pl.ds(0,128),:]=R.T
            l_ref[:,blk]=lcol[pl.ds(pl.multiple_of((lax.bitwise_and(strip,1))*64,64),64),:]
        mh,ml=split(M)
        pan=buf[blk,:]
        ph,plo=split(pan)
        pan=dotg(mh,ph,1,0)+(dotg(mh,plo,1,0)+dotg(ml,ph,1,0))
        buf[blk,:]=pan
        buf[blk,blk]=M
        for kk in range(nb-1):
            @pl.when(k==kk)
            def _():
                n0=128*(kk+1)
                low=buf[n0:,kk*128:kk*128+128]
                lh,ll=split(low)
                lc=dotg(lh,mh,1,1)+(dotg(lh,ml,1,1)+dotg(ll,mh,1,1))
                lcol[n0:,:]=lc
                ch,cl=split(lc)
                lhs=jnp.concatenate([ch,cl,ch],1)
                qh,ql=split(buf[kk*128:kk*128+128,:])
                rhs=jnp.concatenate([qh,qh,ql],0)
                buf[n0:,kk*128:kk*128+128]=jnp.zeros((N-n0,128),F32)
                buf[n0:,:]=buf[n0:,:]-dotg(lhs,rhs,1,0)
        @pl.when(k<b)
        def _():
            l_ref[:,blk]=lcol[pl.ds(pl.multiple_of(strip*64,64),64),:]
        return 0
    lax.fori_loop(0,nb,step,0)
    for k in range(nb):
        n1=128*(k+1)
        m_ref[k*128:n1,:n1]=buf[k*128:n1,:n1].astype(BF)

def chol(who,mine,other):
    return pl.pallas_call(chol_kernel,
        out_shape=(jax.ShapeDtypeStruct((64,1024),F32),jax.ShapeDtypeStruct((1024,1024),BF)),
        in_specs=[pl.BlockSpec(memory_space=pltpu.SMEM)]+[pl.BlockSpec(memory_space=pltpu.VMEM)]*2,
        out_specs=(pl.BlockSpec(memory_space=pltpu.VMEM),)*2,
        scratch_shapes=[pltpu.VMEM((1024,1024),F32),pltpu.VMEM((1024,128),F32)],
        compiler_params=pltpu.CompilerParams(vmem_limit_bytes=18*2**20),
        name="chol_inverse",cost_estimate=pl.CostEstimate(flops=3*10**10,bytes_accessed=5*10**6,transcendentals=1024))(who,mine,other)


def cols(shape,axis): return lax.broadcasted_iota(jnp.int32,shape,axis)

def pair(a,b,ca):
    n=b.shape[1]
    h,l=split(b)
    both=dotg(a,jnp.concatenate([h,l],1),ca,0)
    return both[:,:n]+both[:,n:]

def early_kernel(trank,krank,tu,tv,om,top_ref):
    top=dotg(tv[...],om[...],0,0)
    live=(cols(top.shape,0)<trank[0])&(cols(top.shape,1)<krank[0])
    top_ref[...]=pair(tu[...],jnp.where(live,top,F32(0)),1)

def finish_kernel(who,m,rcat,ccat,tu,tv,om,top,row_ref,col_ref,nu_ref,nv_ref,rw,cw):
    ru=rcat.at[:,:256]; rv=rcat.at[:,256:]; cu=ccat.at[:,:256]; cv=ccat.at[:,256:]
    rr,cr,tr,kr=who[0],who[1],who[2],who[3]
    i=who[4]; j=who[5]
    for b in range(4):
        s=slice(256*b,256*b+256); e=256*b+256
        acc=dotg(m[s,:e],rv[:e,:],1,0)
        rw[s,:]=jnp.where(cols(acc.shape,1)<rr,acc,F32(0)).astype(BF)
        acc=dotg(m[s,:e],cv[:e,:],1,0)
        cw[s,:]=jnp.where(cols(acc.shape,1)<cr,acc,F32(0)).astype(BF)
    row_ref[...]=rw[pl.ds(pl.multiple_of(j*32,32),32),:]
    col_ref[...]=cw[pl.ds(pl.multiple_of(i*64,64),64),:]
    couple=dotg(rw[...],cw[...],0,0)
    low=dotg(cu[...],om[...],0,0)
    low=jnp.where(cols(low.shape,1)<kr,low,F32(0))
    mixed=dot3(couple,low,1,0)
    sample=top[...]-pair(ru[...],mixed,1)
    gram=dot3(sample,sample,0,0)
    eye=(cols(gram.shape,0)==cols(gram.shape,1))&(cols(gram.shape,0)>=kr)
    gram=gram+jnp.where(eye,F32(1),F32(0))
    _,W=factor([gram[8*g:8*g+8,:] for g in range(16)])
    W=jnp.concatenate(W,0)
    q=dot3(sample,W,1,1)
    nu_ref[...]=(q*F32(32)).astype(BF)
    ptop=pair(tu[...],q,0)
    ptop=jnp.where(cols(ptop.shape,0)<tr,ptop,F32(0))
    rproj=pair(ru[...],q,0)
    plow=dot3(couple,rproj,0,0)
    nv_ref[...]=(pair(tv[...],ptop,1)-pair(cu[...],plow,1)).astype(BF)

def early(trank,krank,tu,tv,om):
    return pl.pallas_call(early_kernel,out_shape=jax.ShapeDtypeStruct((1024,128),F32),
        in_specs=[pl.BlockSpec(memory_space=pltpu.SMEM)]*2+[pl.BlockSpec(memory_space=pltpu.VMEM)]*3,
        out_specs=pl.BlockSpec(memory_space=pltpu.VMEM),
        compiler_params=pltpu.CompilerParams(vmem_limit_bytes=16*2**20),name="early_sample")(trank,krank,tu,tv,om)

def finish(who,m,rcat,ccat,tu,tv,om,top):
    return pl.pallas_call(finish_kernel,
        out_shape=(jax.ShapeDtypeStruct((32,256),BF),jax.ShapeDtypeStruct((64,256),BF),
                   jax.ShapeDtypeStruct((1024,128),BF),jax.ShapeDtypeStruct((1024,128),BF)),
        in_specs=[pl.BlockSpec(memory_space=pltpu.SMEM)]+[pl.BlockSpec(memory_space=pltpu.VMEM)]*7,
        out_specs=(pl.BlockSpec(memory_space=pltpu.VMEM),)*4,
        scratch_shapes=[pltpu.VMEM((1024,256),BF)]*2,
        compiler_params=pltpu.CompilerParams(vmem_limit_bytes=24*2**20),name="recompress")(who,m,rcat,ccat,tu,tv,om,top)


def to_all(block):
    every=jnp.broadcast_to(block[None],(16,)+block.shape)
    return lax.all_to_all(every,"row",split_axis=0,concat_axis=0,tiled=True)


def per_device(diag_tile,row_u,row_v,col_u,col_v,tile_u,tile_v,omega,row_rank,col_rank,tile_rank,keep_rank):
    i=lax.axis_index("row").astype(jnp.int32); j=lax.axis_index("col").astype(jnp.int32)
    trank=tile_rank.reshape((1,)); krank=keep_rank.reshape((1,))
    tu=tile_u.reshape((1024,256)); tv=tile_v.reshape((1024,256))
    rcat=lax.all_gather(jnp.concatenate([row_u[0],row_v[0]],1),"col",axis=0,tiled=True)
    half=lax.dynamic_slice_in_dim(diag_tile,lax.bitwise_and(j,1)*32,32,0)
    mine=to_all(half)
    other=lax.ppermute(mine,"col",[(s,s^1) for s in range(32)])
    ccat=to_all(jnp.concatenate([col_u[0],col_v[0]],1)).reshape((1024,512))
    top=early(trank,krank,tu,tv,omega)
    strip,inverse=chol(jnp.stack([i,j]),mine,other)
    who=jnp.concatenate([row_rank,col_rank,trank,krank,i[None],j[None]])
    row_out,col_out,new_u,new_v=finish(who,inverse,rcat,ccat,tu,tv,omega,top)
    return (strip,row_out[None],col_out[None],new_u[None,None],new_v[None,None])


def solution(mesh):
    return jax.shard_map(
        per_device,
        mesh=mesh,
        in_specs=(P("row",None),P("row","col",None),P("row","col",None),P("col","row",None),P("col","row",None),
            P("row","col",None,None),P("row","col",None,None),P(),P("row"),P("col"),P("row","col"),P("row","col")),
        out_specs=(P("row",None),P("row","col",None),P("col","row",None),P("row","col",None,None),P("row","col",None,None)),
        check_vma=False)
```

```python
import jax, jax.numpy as jnp
from jax import lax
from jax.sharding import PartitionSpec as P
from jax.experimental import pallas as pl
from jax.experimental.pallas import tpu as pltpu
F32=jnp.float32; BF=jnp.bfloat16
G=8

def lane(x,c): return jnp.broadcast_to(x[:,c:c+1],(8,128))
def sub(x,s): return jnp.broadcast_to(x[s:s+1,:],(8,128))

AHEAD=2


def factor(S):
    row=lax.broadcasted_iota(jnp.int32,(8,128),0); col=lax.broadcasted_iota(jnp.int32,(8,128),1)
    W=[jnp.where(col==row+8*g,F32(1),F32(0)) for g in range(16)]
    S=list(S)
    late=None
    ahead=None
    for p in range(16):
        C=[lane(S[p],8*p+j) for j in range(8)] if ahead is None else ahead
        if late is not None:
            for g in range(p+AHEAD,16):
                S[g]=S[g]-late[8*g:8*g+8,:128]; W[g]=W[g]-late[8*g:8*g+8,128:]
        near=range(p+1,min(p+1+AHEAD+(1-p%2),16))
        T={g:[lane(S[g],8*p+j) for j in range(8)] for g in near}
        ahead=[lane(S[p+1],8*p+8+j) for j in range(8)] if p<15 else None
        a=[[sub(C[j],i) if i>=j else None for j in range(8)] for i in range(8)]
        B=[sub(S[p],j) for j in range(8)]; V=[sub(W[p],j) for j in range(8)]
        for j in range(8):
            r=lax.rsqrt(a[j][j])
            l=[None]*8
            for i in range(j+1,8): l[i]=a[i][j]*r
            for i in range(j+1,8):
                for k in range(j+1,i+1): a[i][k]=a[i][k]-l[i]*l[k]
            for X in [B,V]+list(T.values()):
                X[j]=X[j]*r
                for i in range(j+1,8): X[i]=X[i]-l[i]*X[j]
        if p<15:
            N=T[p+1]
            for k in range(8):
                for j in range(8): ahead[k]=ahead[k]-N[j]*sub(N[j],k)
        S[p]=B[0]; W[p]=V[0]
        for j in range(1,8):
            S[p]=jnp.where(row==j,B[j],S[p]); W[p]=jnp.where(row==j,V[j],W[p])
        for g in near:
            t=[T[g][j]*B[j] for j in range(8)]; u=[T[g][j]*V[j] for j in range(8)]
            S[g]=S[g]-(((t[0]+t[1])+(t[2]+t[3]))+((t[4]+t[5])+(t[6]+t[7])))
            W[g]=W[g]-(((u[0]+u[1])+(u[2]+u[3]))+((u[4]+u[5])+(u[6]+u[7])))
        late=None
        if p%2 and p+1+AHEAD<16:
            both=[jnp.concatenate([S[g],W[g]],1) for g in (p-1,p)]
            high=[x.astype(BF).astype(F32) for x in both]
            low=[x-h for x,h in zip(both,high)]
            left=[x[:,:128] for x in high]
            lhs=jnp.concatenate(left+[x[:,:128] for x in low]+left,0).astype(BF)
            rhs=jnp.concatenate(high+high+low,0).astype(BF)
            late=dotg(lhs,rhs,0,0)
    return S,W


def split(x):
    h=x.astype(BF); return h,(x-h.astype(F32)).astype(BF)
def dotg(a,b,ca,cb): return lax.dot_general(a,b,(((ca,),(cb,)),((),())),preferred_element_type=F32)
def dot3(a,b,ca,cb):
    ah,al=split(a); bh,bl=split(b)
    return dotg(ah,bh,ca,cb)+(dotg(ah,bl,ca,cb)+dotg(al,bh,ca,cb))

def chol_kernel(mine_any,other_any,l_ref,m_ref,buf,lout,mine,other,sems):
    N=1024; nb=8
    strip=lax.axis_index("row").astype(jnp.int32)
    c=lax.bitwise_and(lax.axis_index("col").astype(jnp.int32),1)*32
    copies=[pltpu.make_async_copy(mine_any,mine,sems.at[0]),pltpu.make_async_copy(other_any,other,sems.at[1])]
    for x in copies: x.start()
    for x in copies: x.wait()
    for s in range(16):
        w=128*(s//2+1)
        buf[pl.ds(pl.multiple_of(64*s+c,32),32),:w]=mine[s,:,:w].astype(F32)
        buf[pl.ds(pl.multiple_of(64*s+32-c,32),32),:w]=other[s,:,:w].astype(F32)
    row=lax.broadcasted_iota(jnp.int32,(8,128),0); col=lax.broadcasted_iota(jnp.int32,(8,128),1)
    D=buf[:128,:128]
    for k in range(nb):
        k0=128*k; n0=k0+128
        S,W=factor([D[8*g:8*g+8,:] for g in range(16)])
        M=jnp.concatenate(W,0)
        mh,ml=split(M)
        m_ref[k0:n0,k0:n0]=mh
        R=jnp.concatenate([jnp.where(col>=row+8*g,S[g],F32(0)) for g in range(16)],0)
        lout[k0:n0,k0:n0]=R.T
        if k:
            ph,plo=split(buf[k0:n0,:k0])
            pan=dotg(mh,ph,1,0)+(dotg(mh,plo,1,0)+dotg(ml,ph,1,0))
            m_ref[k0:n0,:k0]=pan.astype(BF)
        if k==nb-1: break
        lout[k0:n0,n0:]=jnp.zeros((128,N-n0),F32)
        m_ref[k0:n0,n0:]=jnp.zeros((128,N-n0),BF)
        lh,ll=split(buf[n0:,k0:n0])
        lc=dotg(lh,mh,1,1)+(dotg(lh,ml,1,1)+dotg(ll,mh,1,1))
        lout[n0:,k0:n0]=lc
        ch,cl=split(lc)
        lhs=jnp.concatenate([ch,cl,ch],1); rhs=jnp.concatenate([ch,ch,cl],1)
        D=buf[n0:n0+128,n0:n0+128]-dotg(lhs[:128],rhs[:128],1,1)
        qh,ql=(mh,ml) if k==0 else split(jnp.concatenate([pan,M],1))
        inv=jnp.concatenate([qh,qh,ql],0)
        up=dotg(lhs,inv,1,0)
        if k: buf[n0:,:k0]=buf[n0:,:k0]-up[:,:k0]
        buf[n0:,k0:n0]=-up[:,k0:]
        for c0 in range(n0+128,N,256):
            c1=min(c0+256,N)
            buf[c0:c1,n0:c1]=buf[c0:c1,n0:c1]-dotg(lhs[c0-n0:c1-n0],rhs[:c1-n0],1,1)
    l_ref[...]=lout[pl.ds(pl.multiple_of(strip*64,64),64),:]

def chol(mine,other):
    return pl.pallas_call(chol_kernel,
        out_shape=(jax.ShapeDtypeStruct((64,1024),F32),jax.ShapeDtypeStruct((1024,1024),BF)),
        in_specs=[pl.BlockSpec(memory_space=pl.ANY)]*2,
        out_specs=(pl.BlockSpec(memory_space=pltpu.VMEM),)*2,
        scratch_shapes=[pltpu.VMEM((1024,1024),F32)]*2+[pltpu.VMEM((16,32,1024),BF)]*2+[pltpu.SemaphoreType.DMA((2,))],
        compiler_params=pltpu.CompilerParams(vmem_limit_bytes=58*2**20),
        name="chol_inverse",cost_estimate=pl.CostEstimate(flops=10**9,bytes_accessed=10**6,transcendentals=1024))(mine,other)


def cols(shape,axis): return lax.broadcasted_iota(jnp.int32,shape,axis)

def pair(a,b,ca):
    n=b.shape[1]
    h,l=split(b)
    both=dotg(a,jnp.concatenate([h,l],1),ca,0)
    return both[:,:n]+both[:,n:]

def finish_kernel(rrank,crank,trank,krank,m_any,rcat_any,ccat_any,tu_any,tv_any,om_any,row_ref,col_ref,nu_ref,nv_ref,
                  rw,cw,rcat,tu,tv,om,m,ccat,sems):
    moves=[pltpu.make_async_copy(x,y,sems.at[n]) for n,(x,y) in enumerate(((ccat_any,ccat),(m_any,m),(rcat_any,rcat),(om_any,om),(tv_any,tv),(tu_any,tu)))]
    for x in moves: x.start()
    rr,cr,tr,kr=rrank[0],crank[0],trank[0,0],krank[0,0]
    i=lax.axis_index("row").astype(jnp.int32); j=lax.axis_index("col").astype(jnp.int32)
    ru=rcat.at[:,:256]; rv=rcat.at[:,256:]; cu=ccat.at[:,:256]; cv=ccat.at[:,256:]
    for x in moves[:2]: x.wait()
    for b in range(4):
        s=slice(256*b,256*b+256); e=256*b+256
        acc=dotg(m[s,:e],cv[:e,:],1,0)
        cw[s,:]=jnp.where(cols(acc.shape,1)<cr,acc,F32(0)).astype(BF)
    for x in moves[2:]: x.wait()
    for b in range(4):
        s=slice(256*b,256*b+256); e=256*b+256
        acc=dotg(m[s,:e],rv[:e,:],1,0)
        rw[s,:]=jnp.where(cols(acc.shape,1)<rr,acc,F32(0)).astype(BF)
    row_ref[...]=rw[pl.ds(pl.multiple_of(j*32,32),32),:]
    col_ref[...]=cw[pl.ds(pl.multiple_of(i*64,64),64),:]
    inner=dotg(tv[...],om[...],0,0)
    inner=jnp.where((cols(inner.shape,0)<tr)&(cols(inner.shape,1)<kr),inner,F32(0))
    top=pair(tu[...],inner,1)
    couple=dotg(rw[...],cw[...],0,0)
    low=dotg(cu[...],om[...],0,0)
    low=jnp.where(cols(low.shape,1)<kr,low,F32(0))
    mixed=dot3(couple,low,1,0)
    sample=top-pair(ru[...],mixed,1)
    gram=dot3(sample,sample,0,0)
    eye=(cols(gram.shape,0)==cols(gram.shape,1))&(cols(gram.shape,0)>=kr)
    gram=gram+jnp.where(eye,F32(1),F32(0))
    _,W=factor([gram[8*g:8*g+8,:] for g in range(16)])
    W=jnp.concatenate(W,0)
    q=dot3(sample,W,1,1)
    nu_ref[...]=(q*F32(32)).astype(BF)
    ptop=pair(tu[...],q,0)
    ptop=jnp.where(cols(ptop.shape,0)<tr,ptop,F32(0))
    rproj=pair(ru[...],q,0)
    plow=dot3(couple,rproj,0,0)
    nv_ref[...]=(pair(tv[...],ptop,1)-pair(cu[...],plow,1)).astype(BF)

def finish(rrank,crank,trank,krank,m,rcat,ccat,tu,tv,om):
    smem=pl.BlockSpec(memory_space=pltpu.SMEM); vmem=pl.BlockSpec(memory_space=pltpu.VMEM); far=pl.BlockSpec(memory_space=pl.ANY)
    return pl.pallas_call(finish_kernel,
        out_shape=(jax.ShapeDtypeStruct((32,256),BF),jax.ShapeDtypeStruct((64,256),BF),
                   jax.ShapeDtypeStruct((1024,128),BF),jax.ShapeDtypeStruct((1024,128),BF)),
        in_specs=[smem]*4+[far]*6,
        out_specs=(vmem,)*4,
        scratch_shapes=[pltpu.VMEM((1024,256),BF)]*2+[pltpu.VMEM((1024,512),BF)]+[pltpu.VMEM((1024,256),BF)]*2
            +[pltpu.VMEM((1024,128),BF),pltpu.VMEM((1024,1024),BF),pltpu.VMEM((1024,512),BF),pltpu.SemaphoreType.DMA((6,))],
        compiler_params=pltpu.CompilerParams(vmem_limit_bytes=58*2**20),name="recompress")(rrank,crank,trank,krank,m,rcat,ccat,tu,tv,om)


def to_all(block):
    every=jnp.broadcast_to(block[None],(16,)+block.shape)
    return lax.all_to_all(every,"row",split_axis=0,concat_axis=0,tiled=True)


def per_device(diag_tile,row_u,row_v,col_u,col_v,tile_u,tile_v,omega,row_rank,col_rank,tile_rank,keep_rank):
    core=lax.bitwise_and(lax.axis_index("col").astype(jnp.int32),1)
    rows=jnp.concatenate([row_u[0],row_v[0]],1)
    half=lax.dynamic_slice_in_dim(diag_tile,core*32,32,0)
    half,rows=lax.optimization_barrier((half,rows))
    rcat=lax.all_gather(rows,"col",axis=0,tiled=True)
    mine=to_all(half)
    other=lax.ppermute(mine,"col",[(s,s^1) for s in range(32)])
    ccat=to_all(jnp.concatenate([col_u[0],col_v[0]],1)).reshape((1024,512))
    strip,inverse=chol(mine,other)
    row_out,col_out,new_u,new_v=finish(row_rank,col_rank,tile_rank,keep_rank,inverse,rcat,ccat,
        tile_u.reshape((1024,256)),tile_v.reshape((1024,256)),omega)
    return (strip,row_out[None],col_out[None],new_u[None,None],new_v[None,None])


def solution(mesh):
    return jax.shard_map(
        per_device,
        mesh=mesh,
        in_specs=(P("row",None),P("row","col",None),P("row","col",None),P("col","row",None),P("col","row",None),
            P("row","col",None,None),P("row","col",None,None),P(),P("row"),P("col"),P("row","col"),P("row","col")),
        out_specs=(P("row",None),P("row","col",None),P("col","row",None),P("row","col",None,None),P("row","col",None,None)),
        check_vma=False)
```

```python
import jax, jax.numpy as jnp
from jax import lax
from jax.sharding import PartitionSpec as P
from jax.experimental import pallas as pl
from jax.experimental.pallas import tpu as pltpu
F32=jnp.float32; BF=jnp.bfloat16
G=8

def lane(x,c): return jnp.broadcast_to(x[:,c:c+1],(8,128))
def sub(x,s): return jnp.broadcast_to(x[s:s+1,:],(8,128))

AHEAD=2


def factor(S):
    row=lax.broadcasted_iota(jnp.int32,(8,128),0); col=lax.broadcasted_iota(jnp.int32,(8,128),1)
    W=[jnp.where(col==row+8*g,F32(1),F32(0)) for g in range(16)]
    S=list(S)
    late=None
    ahead=None
    for p in range(16):
        C=[lane(S[p],8*p+j) for j in range(8)] if ahead is None else ahead
        if late is not None:
            for g in range(p+AHEAD,16):
                S[g]=S[g]-late[8*g:8*g+8,:128]; W[g]=W[g]-late[8*g:8*g+8,128:]
        near=range(p+1,min(p+1+AHEAD+(1-p%2),16))
        T={g:[lane(S[g],8*p+j) for j in range(8)] for g in near}
        ahead=[lane(S[p+1],8*p+8+j) for j in range(8)] if p<15 else None
        a=[[sub(C[j],i) if i>=j else None for j in range(8)] for i in range(8)]
        B=[sub(S[p],j) for j in range(8)]; V=[sub(W[p],j) for j in range(8)]
        for j in range(8):
            r=lax.rsqrt(a[j][j])
            l=[None]*8
            for i in range(j+1,8): l[i]=a[i][j]*r
            for i in range(j+1,8):
                for k in range(j+1,i+1): a[i][k]=a[i][k]-l[i]*l[k]
            for X in [B,V]+list(T.values()):
                X[j]=X[j]*r
                for i in range(j+1,8): X[i]=X[i]-l[i]*X[j]
        if p<15:
            N=T[p+1]
            for k in range(8):
                for j in range(8): ahead[k]=ahead[k]-N[j]*sub(N[j],k)
        S[p]=B[0]; W[p]=V[0]
        for j in range(1,8):
            S[p]=jnp.where(row==j,B[j],S[p]); W[p]=jnp.where(row==j,V[j],W[p])
        for g in near:
            t=[T[g][j]*B[j] for j in range(8)]; u=[T[g][j]*V[j] for j in range(8)]
            S[g]=S[g]-(((t[0]+t[1])+(t[2]+t[3]))+((t[4]+t[5])+(t[6]+t[7])))
            W[g]=W[g]-(((u[0]+u[1])+(u[2]+u[3]))+((u[4]+u[5])+(u[6]+u[7])))
        late=None
        if p%2 and p+1+AHEAD<16:
            both=[jnp.concatenate([S[g],W[g]],1) for g in (p-1,p)]
            high=[x.astype(BF).astype(F32) for x in both]
            low=[x-h for x,h in zip(both,high)]
            left=[x[:,:128] for x in high]
            lhs=jnp.concatenate(left+[x[:,:128] for x in low]+left,0).astype(BF)
            rhs=jnp.concatenate(high+high+low,0).astype(BF)
            late=dotg(lhs,rhs,0,0)
    return S,W


def split(x):
    h=x.astype(BF); return h,(x-h.astype(F32)).astype(BF)
def dotg(a,b,ca,cb): return lax.dot_general(a,b,(((ca,),(cb,)),((),())),preferred_element_type=F32)
def dot3(a,b,ca,cb):
    ah,al=split(a); bh,bl=split(b)
    return dotg(ah,bh,ca,cb)+(dotg(ah,bl,ca,cb)+dotg(al,bh,ca,cb))

def chol_kernel(mine_any,other_any,l_ref,m_ref,buf,lout,mine,other,sems):
    N=1024; nb=8
    strip=lax.axis_index("row").astype(jnp.int32)
    c=lax.bitwise_and(lax.axis_index("col").astype(jnp.int32),1)*32
    copies=[pltpu.make_async_copy(mine_any,mine,sems.at[0]),pltpu.make_async_copy(other_any,other,sems.at[1])]
    for x in copies: x.start()
    for x in copies: x.wait()
    for s in range(16):
        w=128*(s//2+1)
        buf[pl.ds(pl.multiple_of(64*s+c,32),32),:w]=mine[s,:,:w].astype(F32)
        buf[pl.ds(pl.multiple_of(64*s+32-c,32),32),:w]=other[s,:,:w].astype(F32)
    row=lax.broadcasted_iota(jnp.int32,(8,128),0); col=lax.broadcasted_iota(jnp.int32,(8,128),1)
    D=buf[:128,:128]
    for k in range(nb):
        k0=128*k; n0=k0+128
        S,W=factor([D[8*g:8*g+8,:] for g in range(16)])
        M=jnp.concatenate(W,0)
        mh,ml=split(M)
        m_ref[k0:n0,k0:n0]=mh
        R=jnp.concatenate([jnp.where(col>=row+8*g,S[g],F32(0)) for g in range(16)],0)
        lout[k0:n0,k0:n0]=R.T
        if k:
            ph,plo=split(buf[k0:n0,:k0])
            pan=dotg(mh,ph,1,0)+(dotg(mh,plo,1,0)+dotg(ml,ph,1,0))
            m_ref[k0:n0,:k0]=pan.astype(BF)
        if k==nb-1: break
        lout[k0:n0,n0:]=jnp.zeros((128,N-n0),F32)
        m_ref[k0:n0,n0:]=jnp.zeros((128,N-n0),BF)
        lh,ll=split(buf[n0:,k0:n0])
        lc=dotg(lh,mh,1,1)+(dotg(lh,ml,1,1)+dotg(ll,mh,1,1))
        lout[n0:,k0:n0]=lc
        ch,cl=split(lc)
        lhs=jnp.concatenate([ch,cl,ch],1); rhs=jnp.concatenate([ch,ch,cl],1)
        D=buf[n0:n0+128,n0:n0+128]-dotg(lhs[:128],rhs[:128],1,1)
        qh,ql=(mh,ml) if k==0 else split(jnp.concatenate([pan,M],1))
        inv=jnp.concatenate([qh,qh,ql],0)
        up=dotg(lhs,inv,1,0)
        if k: buf[n0:,:k0]=buf[n0:,:k0]-up[:,:k0]
        buf[n0:,k0:n0]=-up[:,k0:]
        for c0 in range(n0+128,N,256):
            c1=min(c0+256,N)
            buf[c0:c1,n0:c1]=buf[c0:c1,n0:c1]-dotg(lhs[c0-n0:c1-n0],rhs[:c1-n0],1,1)
    l_ref[...]=lout[pl.ds(pl.multiple_of(strip*64,64),64),:]

def chol(mine,other):
    return pl.pallas_call(chol_kernel,
        out_shape=(jax.ShapeDtypeStruct((64,1024),F32),jax.ShapeDtypeStruct((1024,1024),BF)),
        in_specs=[pl.BlockSpec(memory_space=pl.ANY)]*2,
        out_specs=(pl.BlockSpec(memory_space=pltpu.VMEM),)*2,
        scratch_shapes=[pltpu.VMEM((1024,1024),F32)]*2+[pltpu.VMEM((16,32,1024),BF)]*2+[pltpu.SemaphoreType.DMA((2,))],
        compiler_params=pltpu.CompilerParams(vmem_limit_bytes=58*2**20),
        name="chol_inverse",cost_estimate=pl.CostEstimate(flops=3*10**10,bytes_accessed=5*10**6,transcendentals=1024))(mine,other)


def cols(shape,axis): return lax.broadcasted_iota(jnp.int32,shape,axis)

def pair(a,b,ca):
    n=b.shape[1]
    h,l=split(b)
    both=dotg(a,jnp.concatenate([h,l],1),ca,0)
    return both[:,:n]+both[:,n:]

def finish_kernel(rrank,crank,trank,krank,m_any,rmine,rother,cblocks,tu_any,tv_any,om_any,row_ref,col_ref,nu_ref,nv_ref,
                  rw,cw,rcat,tu,tv,om,m,ccat,sems):
    rr,cr,tr,kr=rrank[0],crank[0],trank[0,0],krank[0,0]
    i=lax.axis_index("row").astype(jnp.int32); j=lax.axis_index("col").astype(jnp.int32)
    c=lax.bitwise_and(j,1)*32
    cmoves=[pltpu.make_async_copy(m_any,m,sems.at[0])]
    for t in range(16):
        at=pl.multiple_of(lax.bitwise_xor(i,jnp.int32(FROM[t]))*64,64)
        cmoves.append(pltpu.make_async_copy(cblocks.at[t],ccat.at[pl.ds(at,64)],sems.at[t+4]))
    rmoves=[pltpu.make_async_copy(x,y,sems.at[n+1]) for n,(x,y) in enumerate(((om_any,om),(tv_any,tv),(tu_any,tu)))]
    for t in range(16):
        rmoves.append(pltpu.make_async_copy(rmine.at[t],rcat.at[pl.ds(pl.multiple_of(64*t+c,32),32)],sems.at[t+20]))
        rmoves.append(pltpu.make_async_copy(rother.at[t],rcat.at[pl.ds(pl.multiple_of(64*t+32-c,32),32)],sems.at[t+36]))
    for x in cmoves+rmoves: x.start()
    ru=rcat.at[:,:256]; rv=rcat.at[:,256:]; cu=ccat.at[:,:256]; cv=ccat.at[:,256:]
    for x in cmoves: x.wait()
    for b in range(4):
        s=slice(256*b,256*b+256); e=256*b+256
        acc=dotg(m[s,:e],cv[:e,:],1,0)
        cw[s,:]=jnp.where(cols(acc.shape,1)<cr,acc,F32(0)).astype(BF)
    for x in rmoves: x.wait()
    for b in range(4):
        s=slice(256*b,256*b+256); e=256*b+256
        acc=dotg(m[s,:e],rv[:e,:],1,0)
        rw[s,:]=jnp.where(cols(acc.shape,1)<rr,acc,F32(0)).astype(BF)
    row_ref[...]=rw[pl.ds(pl.multiple_of(j*32,32),32),:]
    col_ref[...]=cw[pl.ds(pl.multiple_of(i*64,64),64),:]
    inner=dotg(tv[...],om[...],0,0)
    inner=jnp.where((cols(inner.shape,0)<tr)&(cols(inner.shape,1)<kr),inner,F32(0))
    top=pair(tu[...],inner,1)
    couple=dotg(rw[...],cw[...],0,0)
    low=dotg(cu[...],om[...],0,0)
    low=jnp.where(cols(low.shape,1)<kr,low,F32(0))
    mixed=dot3(couple,low,1,0)
    sample=top-pair(ru[...],mixed,1)
    gram=dot3(sample,sample,0,0)
    eye=(cols(gram.shape,0)==cols(gram.shape,1))&(cols(gram.shape,0)>=kr)
    gram=gram+jnp.where(eye,F32(1),F32(0))
    _,W=factor([gram[8*g:8*g+8,:] for g in range(16)])
    W=jnp.concatenate(W,0)
    q=dot3(sample,W,1,1)
    nu_ref[...]=(q*F32(32)).astype(BF)
    ptop=pair(tu[...],q,0)
    ptop=jnp.where(cols(ptop.shape,0)<tr,ptop,F32(0))
    rproj=pair(ru[...],q,0)
    plow=dot3(couple,rproj,0,0)
    nv_ref[...]=(pair(tv[...],ptop,1)-pair(cu[...],plow,1)).astype(BF)

def finish(rrank,crank,trank,krank,m,rmine,rother,cblocks,tu,tv,om):
    smem=pl.BlockSpec(memory_space=pltpu.SMEM); vmem=pl.BlockSpec(memory_space=pltpu.VMEM); far=pl.BlockSpec(memory_space=pl.ANY)
    return pl.pallas_call(finish_kernel,
        out_shape=(jax.ShapeDtypeStruct((32,256),BF),jax.ShapeDtypeStruct((64,256),BF),
                   jax.ShapeDtypeStruct((1024,128),BF),jax.ShapeDtypeStruct((1024,128),BF)),
        in_specs=[smem]*4+[far]*7,
        out_specs=(vmem,)*4,
        scratch_shapes=[pltpu.VMEM((1024,256),BF)]*2+[pltpu.VMEM((1024,512),BF)]+[pltpu.VMEM((1024,256),BF)]*2
            +[pltpu.VMEM((1024,128),BF),pltpu.VMEM((1024,1024),BF),pltpu.VMEM((1024,512),BF),pltpu.SemaphoreType.DMA((52,))],
        compiler_params=pltpu.CompilerParams(vmem_limit_bytes=58*2**20),name="recompress")(rrank,crank,trank,krank,m,rmine,rother,cblocks,tu,tv,om)


SAME_CORE=[list(range(0,32,2)),list(range(1,32,2))]
STEPS=(1,3,4,12)
FROM=[0]
for _m in STEPS: FROM=FROM+[f^_m for f in FROM]


def to_all(block,axis,groups=None):
    every=jnp.broadcast_to(block[None],(16,)+block.shape)
    return lax.all_to_all(every,axis,split_axis=0,concat_axis=0,axis_index_groups=groups,tiled=True)


def other_core(block):
    return lax.ppermute(block,"col",[(s,s^1) for s in range(32)])


def doubled(have,mask):
    return jnp.concatenate([have,lax.ppermute(have,"row",[(s,s^mask) for s in range(16)])],0)


def per_device(diag_tile,row_u,row_v,col_u,col_v,tile_u,tile_v,omega,row_rank,col_rank,tile_rank,keep_rank):
    core=lax.bitwise_and(lax.axis_index("col").astype(jnp.int32),1)
    half=lax.dynamic_slice_in_dim(diag_tile,core*32,32,0)
    mine=to_all(half,"row")
    cblocks=jnp.concatenate([col_u[0],col_v[0]],1)[None]
    cblocks=doubled(cblocks,STEPS[0])
    mine,cblocks=lax.optimization_barrier((mine,cblocks))
    other=other_core(mine)
    for mask in STEPS[1:3]: cblocks=doubled(cblocks,mask)
    other,cblocks=lax.optimization_barrier((other,cblocks))
    cblocks=doubled(cblocks,STEPS[3])
    rmine=to_all(jnp.concatenate([row_u[0],row_v[0]],1),"col",SAME_CORE)
    strip,inverse=chol(mine,other)
    rmine,inverse=lax.optimization_barrier((rmine,inverse))
    rother=other_core(rmine)
    row_out,col_out,new_u,new_v=finish(row_rank,col_rank,tile_rank,keep_rank,inverse,rmine,rother,cblocks,
        tile_u.reshape((1024,256)),tile_v.reshape((1024,256)),omega)
    return (strip,row_out[None],col_out[None],new_u[None,None],new_v[None,None])


def solution(mesh):
    return jax.shard_map(
        per_device,
        mesh=mesh,
        in_specs=(P("row",None),P("row","col",None),P("row","col",None),P("col","row",None),P("col","row",None),
            P("row","col",None,None),P("row","col",None,None),P(),P("row"),P("col"),P("row","col"),P("row","col")),
        out_specs=(P("row",None),P("row","col",None),P("col","row",None),P("row","col",None,None),P("row","col",None,None)),
        check_vma=False)
```

```python
import jax, jax.numpy as jnp
from jax import lax
from jax.sharding import PartitionSpec as P
from jax.experimental import pallas as pl
from jax.experimental.pallas import tpu as pltpu
F32=jnp.float32; BF=jnp.bfloat16
G=8

def lane(x,c): return jnp.broadcast_to(x[:,c:c+1],(8,128))
def sub(x,s): return jnp.broadcast_to(x[s:s+1,:],(8,128))

AHEAD=2


def factor(S):
    row=lax.broadcasted_iota(jnp.int32,(8,128),0); col=lax.broadcasted_iota(jnp.int32,(8,128),1)
    W=[jnp.where(col==row+8*g,F32(1),F32(0)) for g in range(16)]
    S=list(S)
    late=None
    ahead=None
    for p in range(16):
        C=[lane(S[p],8*p+j) for j in range(8)] if ahead is None else ahead
        if late is not None:
            for g in range(p+AHEAD,16):
                S[g]=S[g]-late[8*g:8*g+8,:128]; W[g]=W[g]-late[8*g:8*g+8,128:]
        near=range(p+1,min(p+1+AHEAD+(1-p%2),16))
        T={g:[lane(S[g],8*p+j) for j in range(8)] for g in near}
        ahead=[lane(S[p+1],8*p+8+j) for j in range(8)] if p<15 else None
        a=[[sub(C[j],i) if i>=j else None for j in range(8)] for i in range(8)]
        B=[sub(S[p],j) for j in range(8)]; V=[sub(W[p],j) for j in range(8)]
        for j in range(8):
            r=lax.rsqrt(a[j][j])
            l=[None]*8
            for i in range(j+1,8): l[i]=a[i][j]*r
            for i in range(j+1,8):
                for k in range(j+1,i+1): a[i][k]=a[i][k]-l[i]*l[k]
            for X in [B,V]+list(T.values()):
                X[j]=X[j]*r
                for i in range(j+1,8): X[i]=X[i]-l[i]*X[j]
        if p<15:
            N=T[p+1]
            for k in range(8):
                for j in range(8): ahead[k]=ahead[k]-N[j]*sub(N[j],k)
        S[p]=B[0]; W[p]=V[0]
        for j in range(1,8):
            S[p]=jnp.where(row==j,B[j],S[p]); W[p]=jnp.where(row==j,V[j],W[p])
        for g in near:
            t=[T[g][j]*B[j] for j in range(8)]; u=[T[g][j]*V[j] for j in range(8)]
            S[g]=S[g]-(((t[0]+t[1])+(t[2]+t[3]))+((t[4]+t[5])+(t[6]+t[7])))
            W[g]=W[g]-(((u[0]+u[1])+(u[2]+u[3]))+((u[4]+u[5])+(u[6]+u[7])))
        late=None
        if p%2 and p+1+AHEAD<16:
            both=[jnp.concatenate([S[g],W[g]],1) for g in (p-1,p)]
            high=[x.astype(BF).astype(F32) for x in both]
            low=[x-h for x,h in zip(both,high)]
            left=[x[:,:128] for x in high]
            lhs=jnp.concatenate(left+[x[:,:128] for x in low]+left,0).astype(BF)
            rhs=jnp.concatenate(high+high+low,0).astype(BF)
            late=dotg(lhs,rhs,0,0)
    return S,W


def split(x):
    h=x.astype(BF); return h,(x-h.astype(F32)).astype(BF)
def dotg(a,b,ca,cb): return lax.dot_general(a,b,(((ca,),(cb,)),((),())),preferred_element_type=F32)
def dot3(a,b,ca,cb):
    ah,al=split(a); bh,bl=split(b)
    return dotg(ah,bh,ca,cb)+(dotg(ah,bl,ca,cb)+dotg(al,bh,ca,cb))

def chol_kernel(mine_any,other_any,l_ref,m_ref,buf,lout,mine,other,sems):
    N=1024; nb=8
    strip=lax.axis_index("row").astype(jnp.int32)
    c=lax.bitwise_and(lax.axis_index("col").astype(jnp.int32),1)*32
    copies=[pltpu.make_async_copy(mine_any,mine,sems.at[0]),pltpu.make_async_copy(other_any,other,sems.at[1])]
    for x in copies: x.start()
    for x in copies: x.wait()
    for s in range(16):
        w=128*(s//2+1)
        buf[pl.ds(pl.multiple_of(64*s+c,32),32),:w]=mine[s,:,:w].astype(F32)
        buf[pl.ds(pl.multiple_of(64*s+32-c,32),32),:w]=other[s,:,:w].astype(F32)
    row=lax.broadcasted_iota(jnp.int32,(8,128),0); col=lax.broadcasted_iota(jnp.int32,(8,128),1)
    D=buf[:128,:128]
    for k in range(nb):
        k0=128*k; n0=k0+128
        S,W=factor([D[8*g:8*g+8,:] for g in range(16)])
        M=jnp.concatenate(W,0)
        mh,ml=split(M)
        m_ref[k0:n0,k0:n0]=mh
        R=jnp.concatenate([jnp.where(col>=row+8*g,S[g],F32(0)) for g in range(16)],0)
        lout[k0:n0,k0:n0]=R.T
        if k:
            ph,plo=split(buf[k0:n0,:k0])
            pan=dotg(mh,ph,1,0)+(dotg(mh,plo,1,0)+dotg(ml,ph,1,0))
            m_ref[k0:n0,:k0]=pan.astype(BF)
        if k==nb-1: break
        lout[k0:n0,n0:]=jnp.zeros((128,N-n0),F32)
        m_ref[k0:n0,n0:]=jnp.zeros((128,N-n0),BF)
        lh,ll=split(buf[n0:,k0:n0])
        lc=dotg(lh,mh,1,1)+(dotg(lh,ml,1,1)+dotg(ll,mh,1,1))
        lout[n0:,k0:n0]=lc
        ch,cl=split(lc)
        lhs=jnp.concatenate([ch,cl,ch],1); rhs=jnp.concatenate([ch,ch,cl],1)
        D=buf[n0:n0+128,n0:n0+128]-dotg(lhs[:128],rhs[:128],1,1)
        qh,ql=(mh,ml) if k==0 else split(jnp.concatenate([pan,M],1))
        inv=jnp.concatenate([qh,qh,ql],0)
        up=dotg(lhs,inv,1,0)
        if k: buf[n0:,:k0]=buf[n0:,:k0]-up[:,:k0]
        buf[n0:,k0:n0]=-up[:,k0:]
        for c0 in range(n0+128,N,256):
            c1=min(c0+256,N)
            buf[c0:c1,n0:c1]=buf[c0:c1,n0:c1]-dotg(lhs[c0-n0:c1-n0],rhs[:c1-n0],1,1)
    l_ref[...]=lout[pl.ds(pl.multiple_of(strip*64,64),64),:]

def chol(mine,other):
    return pl.pallas_call(chol_kernel,
        out_shape=(jax.ShapeDtypeStruct((64,1024),F32),jax.ShapeDtypeStruct((1024,1024),BF)),
        in_specs=[pl.BlockSpec(memory_space=pl.ANY)]*2,
        out_specs=(pl.BlockSpec(memory_space=pltpu.VMEM),)*2,
        scratch_shapes=[pltpu.VMEM((1024,1024),F32)]*2+[pltpu.VMEM((16,32,1024),BF)]*2+[pltpu.SemaphoreType.DMA((2,))],
        compiler_params=pltpu.CompilerParams(vmem_limit_bytes=58*2**20),
        name="chol_inverse",cost_estimate=pl.CostEstimate(flops=3*10**10,bytes_accessed=5*10**6,transcendentals=1024))(mine,other)


def cols(shape,axis): return lax.broadcasted_iota(jnp.int32,shape,axis)

def pair(a,b,ca):
    n=b.shape[1]
    h,l=split(b)
    both=dotg(a,jnp.concatenate([h,l],1),ca,0)
    return both[:,:n]+both[:,n:]

def finish_kernel(rrank,crank,trank,krank,m_any,rmine,rother,cfirst,clast,tu_any,tv_any,om_any,row_ref,col_ref,nu_ref,nv_ref,
                  rw,cw,rcat,tu,tv,om,m,ccat,sems):
    rr,cr,tr,kr=rrank[0],crank[0],trank[0,0],krank[0,0]
    i=lax.axis_index("row").astype(jnp.int32); j=lax.axis_index("col").astype(jnp.int32)
    c=lax.bitwise_and(j,1)*32
    cmoves=[pltpu.make_async_copy(m_any,m,sems.at[0])]
    for t in range(16):
        at=pl.multiple_of(lax.bitwise_xor(i,jnp.int32(FROM[t]))*64,64)
        cmoves.append(pltpu.make_async_copy((cfirst if t<8 else clast).at[t%8],ccat.at[pl.ds(at,64)],sems.at[t+4]))
    rmoves=[pltpu.make_async_copy(x,y,sems.at[n+1]) for n,(x,y) in enumerate(((om_any,om),(tv_any,tv),(tu_any,tu)))]
    for t in range(16):
        rmoves.append(pltpu.make_async_copy(rmine.at[t],rcat.at[pl.ds(pl.multiple_of(64*t+c,32),32)],sems.at[t+20]))
        rmoves.append(pltpu.make_async_copy(rother.at[t],rcat.at[pl.ds(pl.multiple_of(64*t+32-c,32),32)],sems.at[t+36]))
    for x in cmoves+rmoves: x.start()
    ru=rcat.at[:,:256]; rv=rcat.at[:,256:]; cu=ccat.at[:,:256]; cv=ccat.at[:,256:]
    for x in cmoves: x.wait()
    for b in range(4):
        s=slice(256*b,256*b+256); e=256*b+256
        acc=dotg(m[s,:e],cv[:e,:],1,0)
        cw[s,:]=jnp.where(cols(acc.shape,1)<cr,acc,F32(0)).astype(BF)
    for x in rmoves: x.wait()
    for b in range(4):
        s=slice(256*b,256*b+256); e=256*b+256
        acc=dotg(m[s,:e],rv[:e,:],1,0)
        rw[s,:]=jnp.where(cols(acc.shape,1)<rr,acc,F32(0)).astype(BF)
    row_ref[...]=rw[pl.ds(pl.multiple_of(j*32,32),32),:]
    col_ref[...]=cw[pl.ds(pl.multiple_of(i*64,64),64),:]
    inner=dotg(tv[...],om[...],0,0)
    inner=jnp.where((cols(inner.shape,0)<tr)&(cols(inner.shape,1)<kr),inner,F32(0))
    top=pair(tu[...],inner,1)
    couple=dotg(rw[...],cw[...],0,0)
    low=dotg(cu[...],om[...],0,0)
    low=jnp.where(cols(low.shape,1)<kr,low,F32(0))
    mixed=dot3(couple,low,1,0)
    sample=top-pair(ru[...],mixed,1)
    gram=dot3(sample,sample,0,0)
    eye=(cols(gram.shape,0)==cols(gram.shape,1))&(cols(gram.shape,0)>=kr)
    gram=gram+jnp.where(eye,F32(1),F32(0))
    _,W=factor([gram[8*g:8*g+8,:] for g in range(16)])
    W=jnp.concatenate(W,0)
    q=dot3(sample,W,1,1)
    nu_ref[...]=(q*F32(32)).astype(BF)
    ptop=pair(tu[...],q,0)
    ptop=jnp.where(cols(ptop.shape,0)<tr,ptop,F32(0))
    rproj=pair(ru[...],q,0)
    plow=dot3(couple,rproj,0,0)
    nv_ref[...]=(pair(tv[...],ptop,1)-pair(cu[...],plow,1)).astype(BF)

def finish(rrank,crank,trank,krank,m,rmine,rother,cfirst,clast,tu,tv,om):
    smem=pl.BlockSpec(memory_space=pltpu.SMEM); vmem=pl.BlockSpec(memory_space=pltpu.VMEM); far=pl.BlockSpec(memory_space=pl.ANY)
    return pl.pallas_call(finish_kernel,
        out_shape=(jax.ShapeDtypeStruct((32,256),BF),jax.ShapeDtypeStruct((64,256),BF),
                   jax.ShapeDtypeStruct((1024,128),BF),jax.ShapeDtypeStruct((1024,128),BF)),
        in_specs=[smem]*4+[far]*8,
        out_specs=(vmem,)*4,
        scratch_shapes=[pltpu.VMEM((1024,256),BF)]*2+[pltpu.VMEM((1024,512),BF)]+[pltpu.VMEM((1024,256),BF)]*2
            +[pltpu.VMEM((1024,128),BF),pltpu.VMEM((1024,1024),BF),pltpu.VMEM((1024,512),BF),pltpu.SemaphoreType.DMA((52,))],
        compiler_params=pltpu.CompilerParams(vmem_limit_bytes=58*2**20),name="recompress")(rrank,crank,trank,krank,m,rmine,rother,cfirst,clast,tu,tv,om)


SAME_CORE=[list(range(0,32,2)),list(range(1,32,2))]
STEPS=(1,3,4,12)
FROM=[0]
for _m in STEPS: FROM=FROM+[f^_m for f in FROM]


def to_all(block,axis,groups=None):
    every=jnp.broadcast_to(block[None],(16,)+block.shape)
    return lax.all_to_all(every,axis,split_axis=0,concat_axis=0,axis_index_groups=groups,tiled=True)


def other_core(block):
    return lax.ppermute(block,"col",[(s,s^1) for s in range(32)])


def exchanged(have,mask):
    return lax.ppermute(have,"row",[(s,s^mask) for s in range(16)])


def doubled(have,mask):
    return jnp.concatenate([have,exchanged(have,mask)],0)


def per_device(diag_tile,row_u,row_v,col_u,col_v,tile_u,tile_v,omega,row_rank,col_rank,tile_rank,keep_rank):
    core=lax.bitwise_and(lax.axis_index("col").astype(jnp.int32),1)
    half=lax.dynamic_slice_in_dim(diag_tile,core*32,32,0)
    mine=to_all(half,"row")
    cblocks=jnp.concatenate([col_u[0],col_v[0]],1)[None]
    cblocks=doubled(cblocks,STEPS[0])
    mine,cblocks=lax.optimization_barrier((mine,cblocks))
    other=other_core(mine)
    for mask in STEPS[1:3]: cblocks=doubled(cblocks,mask)
    other,cblocks=lax.optimization_barrier((other,cblocks))
    clast=exchanged(cblocks,STEPS[3])
    rmine=to_all(jnp.concatenate([row_u[0],row_v[0]],1),"col",SAME_CORE)
    strip,inverse=chol(mine,other)
    rmine,inverse,clast=lax.optimization_barrier((rmine,inverse,clast))
    rother=other_core(rmine)
    row_out,col_out,new_u,new_v=finish(row_rank,col_rank,tile_rank,keep_rank,inverse,rmine,rother,cblocks,clast,
        tile_u.reshape((1024,256)),tile_v.reshape((1024,256)),omega)
    return (strip,row_out[None],col_out[None],new_u[None,None],new_v[None,None])


def solution(mesh):
    return jax.shard_map(
        per_device,
        mesh=mesh,
        in_specs=(P("row",None),P("row","col",None),P("row","col",None),P("col","row",None),P("col","row",None),
            P("row","col",None,None),P("row","col",None,None),P(),P("row"),P("col"),P("row","col"),P("row","col")),
        out_specs=(P("row",None),P("row","col",None),P("col","row",None),P("row","col",None,None),P("row","col",None,None)),
        check_vma=False)
```
